32 devices in a mesh: section: 2 (over x), lat: 8 (over z, y), lon: 2 (over core).
Axes of the slice: x: 2, y: 2, z: 4, core: 2. Of those that a mesh axis runs over, the one named last changes fastest.
Arguments:
- block_hidden: bfloat16 [2, 48, 768, 512], P('section', 'lat', 'lon'), may hold values from -6 to 6
- incoming_grad: bfloat16 [2, 48, 768, 512], P('section', 'lat', 'lon'), may hold values from -6 to 6
- saved_coeffs: bfloat16 [2, 2, 384, 384, 512], P('section', None, None, 'lat', 'lon'), may hold values from -6 to 6
- filter_weights: float32 [2, 2, 384, 512], P('section', None, None, 'lon'), may hold values from -6 to 6
- up_weight: bfloat16 [2, 512, 512], P('section'), may hold values from -0.25 to 0.25
- down_weight: bfloat16 [2, 512, 512], P('section'), may hold values from -0.25 to 0.25
- latitude_maps: bfloat16 [384, 384, 48], P('lat'), may hold values from -0.3125 to 0.3125
Outputs:
- handed_grad: bfloat16 [2, 48, 768, 512], P('section', 'lat', 'lon')
- filter_grad: float32 [2, 2, 384, 512], P('section', None, 'lat', 'lon')
- up_grad: float32 [2, 512, 512], P('section', ('lat', 'lon'))
- down_grad: float32 [2, 512, 512], P('section', ('lat', 'lon'))
The draws below stay inside these ranges and needn't reach their ends.
All inputs are finite; a program needn't handle non-finite values.
Results may differ from the reference program's by a relative error of at most 0.0085.
Values may be sent and summed in bfloat16 or wider, within the bound.
A program may use at most 256 MiB of HBM per device.

```python
import math
import jax
import jax.numpy as jnp
from jax import lax

EMBED = 512
HIDDEN_SIZE = 512
NLON = 768
MODES = 384
DEGREES = 384
NLAT = 48
SECTIONS = 2


def shard_levels(stream_key, extent, shards, smallest, largest):
    def one(position, shards_of):
        draws = jax.random.uniform(jax.random.fold_in(jax.random.fold_in(stream_key, 6), position), (shards_of,), jnp.float32, smallest / len(shards), largest / len(shards))
        return jnp.repeat(jnp.exp(draws), extent[position] // shards_of).reshape((-1,) + (1,) * (len(extent) - position - 1))

    factor_of = one(*shards[0])
    for cut in shards[1:]:
        factor_of = factor_of * one(*cut)
    return factor_of


def normal_values(own_key, dims, width, limit, split=(), held_as=jnp.bfloat16):
    result = jax.random.normal(own_key, dims, jnp.float32) * width
    if len(split) > 0:
        result = shard_levels(own_key, dims, split, -0.22, 0.18) * result
    return jnp.clip(result, min=-limit, max=limit).astype(held_as)


def setup_inputs(seed: int = 0) -> dict:
    key_of = jax.random.split(jax.random.key(seed), 8)
    return {
        "block_hidden": normal_values(key_of[0], (SECTIONS, NLAT, NLON, EMBED), 1.0, 6.0, ((0, 2), (1, 8), (2, 2))),
        "incoming_grad": normal_values(key_of[1], (SECTIONS, NLAT, NLON, EMBED), 1.0, 6.0, ((0, 2), (1, 8), (2, 2))),
        "saved_coeffs": normal_values(key_of[2], (SECTIONS, 2, DEGREES, MODES, EMBED), 1.0, 6.0, ((0, 2), (3, 8), (4, 2))),
        "filter_weights": normal_values(key_of[3], (SECTIONS, 2, DEGREES, EMBED), 1.0, 6.0, ((0, 2), (3, 2)), jnp.float32),
        "up_weight": normal_values(key_of[4], (SECTIONS, EMBED, HIDDEN_SIZE), EMBED ** -0.5, 0.25, ((0, 2),)),
        "down_weight": normal_values(key_of[5], (SECTIONS, HIDDEN_SIZE, EMBED), HIDDEN_SIZE ** -0.5, 0.25, ((0, 2),)),
        "latitude_maps": normal_values(key_of[6], (MODES, DEGREES, NLAT), DEGREES ** -0.5, 0.3125, ((0, 8),)),
    }


def transform_tables(offset, length, period, orders_kept):
    positions = offset + jnp.arange(length, dtype=jnp.int32)
    orders = jnp.arange(orders_kept, dtype=jnp.int32)
    phases = positions[:, None] * orders[None, :] % period
    angles = phases.astype(jnp.float32) * (2.0 * math.pi / period)
    factor = 1.0 / math.sqrt(period)
    cosine = jnp.cos(angles) * factor
    sine_part = jnp.sin(angles) * factor
    doubled = jnp.where(orders == 0, 1.0, 2.0).astype(jnp.float32)[None, :]
    synthesis = jnp.stack([cosine * doubled, -sine_part * doubled]).astype(jnp.bfloat16)
    analysis = jnp.stack([cosine, -sine_part]).astype(jnp.bfloat16)
    return (synthesis, analysis)

def gelu_pair(pre_active):
    normal_cdf = 0.5 * (1.0 + lax.erf(pre_active * (1.0 / math.sqrt(2.0))))
    density = jnp.exp(-0.5 * pre_active * pre_active) * (1.0 / math.sqrt(2.0 * math.pi))
    return (pre_active * normal_cdf, normal_cdf + pre_active * density)

def mixer_backward(block_rows, grad_rows, up_matrix, down_matrix):

    def one_band(totals, inputs):
        up_total, down_total = totals
        input_band, grad_band = inputs
        pre_active = jnp.dot(input_band, up_matrix, preferred_element_type=jnp.float32)
        activation, slopes = gelu_pair(pre_active)
        activated = activation.astype(jnp.bfloat16)
        carried = lax.dot_general(grad_band, down_matrix, (((1,), (1,)), ((), ())), preferred_element_type=jnp.float32)
        grad_pre = (carried * slopes).astype(jnp.bfloat16)
        down_total = down_total + lax.dot_general(activated, grad_band, (((0,), (0,)), ((), ())), preferred_element_type=jnp.float32)
        up_total = up_total + lax.dot_general(input_band, grad_pre, (((0,), (0,)), ((), ())), preferred_element_type=jnp.float32)
        back_band = lax.dot_general(grad_pre, up_matrix, (((1,), (1,)), ((), ())), preferred_element_type=jnp.float32)
        hidden_band = (grad_band.astype(jnp.float32) + back_band).astype(jnp.bfloat16)
        return ((up_total, down_total), hidden_band)
    start_totals = (jnp.zeros((EMBED, HIDDEN_SIZE), jnp.float32), jnp.zeros((HIDDEN_SIZE, EMBED), jnp.float32))
    totals, grad_hidden = lax.scan(one_band, start_totals, (block_rows, grad_rows))
    return (totals[0], totals[1], grad_hidden)

def spectral_backward(grad_hidden, saved, weights, maps_table):
    synthesis, analysis = transform_tables(0, NLON, NLON, MODES)
    spectrum = jnp.einsum('tkc,rkm->rtmc', grad_hidden.astype(jnp.float32), synthesis.astype(jnp.float32)).astype(jnp.bfloat16)
    maps_wide = maps_table.astype(jnp.float32)
    degree_grad = jnp.einsum('mlt,rtmc->rlmc', maps_wide, spectrum.astype(jnp.float32))
    coeffs_wide = saved.astype(jnp.float32)
    filter_terms = jnp.stack([lax.optimization_barrier(jnp.sum(degree_grad[0] * coeffs_wide[0] + degree_grad[1] * coeffs_wide[1], axis=1)), lax.optimization_barrier(jnp.sum(degree_grad[1] * coeffs_wide[0] - degree_grad[0] * coeffs_wide[1], axis=1))])
    weight_real = weights[0][:, None, :]
    weight_imag = weights[1][:, None, :]
    coef_grad = jnp.stack([weight_real * degree_grad[0] + weight_imag * degree_grad[1], weight_real * degree_grad[1] - weight_imag * degree_grad[0]]).astype(jnp.bfloat16)
    band_grad = jnp.einsum('mlt,rlmc->rtmc', maps_wide, coef_grad.astype(jnp.float32)).astype(jnp.bfloat16)
    grid_back = jnp.einsum('rtmc,rkm->tkc', band_grad.astype(jnp.float32), analysis.astype(jnp.float32)).astype(jnp.bfloat16)
    return (filter_terms, grid_back)

def reference(block_hidden, incoming_grad, saved_coeffs, filter_weights, up_weight, down_weight, latitude_maps):
    passed_list = []
    filter_list = []
    up_list = []
    down_list = []
    for section_number in range(SECTIONS):
        up_total, down_total, grad_hidden = mixer_backward(block_hidden[section_number], incoming_grad[section_number], up_weight[section_number], down_weight[section_number])
        filter_terms, grid_back = spectral_backward(grad_hidden, saved_coeffs[section_number], filter_weights[section_number], latitude_maps)
        passed = (grad_hidden.astype(jnp.float32) + grid_back.astype(jnp.float32)).astype(jnp.bfloat16)
        passed_list.append(passed)
        filter_list.append(filter_terms)
        up_list.append(up_total)
        down_list.append(down_total)
    handed_grad = jnp.roll(jnp.stack(passed_list), 1, axis=0)
    return (handed_grad, jnp.stack(filter_list), jnp.stack(up_list), jnp.stack(down_list))
```

```python
import functools
import math

import jax
import jax.numpy as jnp
from jax import lax
from jax.experimental import pallas as pl
from jax.experimental.pallas import tpu as pltpu
from jax.sharding import PartitionSpec as P

MODES = 384


def shifted(block, axis, distance):
    devices = range(lax.axis_size(axis))
    route = [((i - distance) % len(devices), i) for i in devices]
    return lax.ppermute(block, axis, route)


def transform_tables(offset, length, period, orders_kept):
    positions = offset + jnp.arange(length, dtype=jnp.int32)
    orders = jnp.arange(orders_kept, dtype=jnp.int32)
    phases = positions[:, None] * orders[None, :] % period
    angles = phases.astype(jnp.float32) * (2.0 * math.pi / period)
    factor = 1.0 / math.sqrt(period)
    cosine = jnp.cos(angles) * factor
    sine_part = jnp.sin(angles) * factor
    doubled = jnp.where(orders == 0, 1.0, 2.0).astype(jnp.float32)[None, :]
    synthesis = jnp.stack([cosine * doubled, -sine_part * doubled]).astype(jnp.bfloat16)
    analysis = jnp.stack([cosine, -sine_part]).astype(jnp.bfloat16)
    return (synthesis, analysis)


def gelu_pair(pre_active):
    normal_cdf = 0.5 * (1.0 + lax.erf(pre_active * (1.0 / math.sqrt(2.0))))
    density = jnp.exp(-0.5 * pre_active * pre_active) * (1.0 / math.sqrt(2.0 * math.pi))
    return (pre_active * normal_cdf, normal_cdf + pre_active * density)

GROUP = 16


def swap_matrix():
    row = lax.broadcasted_iota(jnp.int32, (GROUP * GROUP, GROUP * GROUP), 0)
    column = lax.broadcasted_iota(jnp.int32, (GROUP * GROUP, GROUP * GROUP), 1)
    partner = row % GROUP * GROUP + row // GROUP
    return jnp.where(partner == column, 1.0, 0.0).astype(jnp.bfloat16)


def swapped(matrix, block):
    flat = block.reshape(GROUP * GROUP, block.shape[2])
    turned = jnp.dot(matrix, flat, preferred_element_type=jnp.float32)
    return turned.astype(jnp.bfloat16).reshape(block.shape)


def middle_group(
    first, x_ref, s_ref, w_ref, map_ref, filter_ref, out_ref, swap_ref, x_major, s_major, out_major
):
    lats, width = x_ref.shape[1], x_ref.shape[3]
    degrees = s_ref.shape[1]
    matrix = swap_ref[...]
    for part in range(2):
        lanes = slice(part * width, (part + 1) * width)
        for piece in range(lats // GROUP):
            rows = slice(piece * GROUP, (piece + 1) * GROUP)
            x_major[:, rows, lanes] = swapped(matrix, x_ref[part, rows])

        @pl.loop(0, degrees // GROUP)
        def _(piece):
            rows = pl.ds(pl.multiple_of(piece * GROUP, GROUP), GROUP)
            s_major[:, rows, lanes] = swapped(matrix, s_ref[part, rows])

    @pl.when(first)
    def _():
        filter_ref[...] = jnp.zeros_like(filter_ref)

    chunk = 128

    @pl.loop(0, GROUP)
    def _(order):
        band = jnp.zeros((lats, 2 * width), jnp.float32)
        bands = x_major[order]
        for start in range(0, degrees, chunk):
            rows = slice(start, start + chunk)
            maps = map_ref[order, :, rows]
            degree = lax.dot_general(
                maps, bands, (((0,), (0,)), ((), ())), preferred_element_type=jnp.float32
            )
            real, imag = degree[:, :width], degree[:, width:]
            saved_real = s_major[order, rows, :width].astype(jnp.float32)
            saved_imag = s_major[order, rows, width:].astype(jnp.float32)
            filter_ref[0, rows] += real * saved_real + imag * saved_imag
            filter_ref[1, rows] += imag * saved_real - real * saved_imag
            weight_real, weight_imag = w_ref[0, rows], w_ref[1, rows]
            coefs = jnp.concatenate(
                [
                    (weight_real * real + weight_imag * imag).astype(jnp.bfloat16),
                    (weight_real * imag - weight_imag * real).astype(jnp.bfloat16),
                ],
                axis=1,
            )
            band = band + jnp.dot(maps, coefs, preferred_element_type=jnp.float32)
        out_major[order] = band.astype(jnp.bfloat16)

    for part in range(2):
        lanes = slice(part * width, (part + 1) * width)
        for piece in range(lats // GROUP):
            rows = slice(piece * GROUP, (piece + 1) * GROUP)
            out_ref[part, rows] = swapped(matrix, out_major[:, rows, lanes])


def middle_kernel(swap_ref, x_ref, s_ref, w_ref, map_ref, filter_ref, out_ref, *scratch):
    middle_group(
        pl.program_id(0) == 0, x_ref, s_ref, w_ref, map_ref, filter_ref, out_ref, swap_ref, *scratch
    )


def middle(order_major, saved, weights, maps):
    _, lats, orders, width = order_major.shape
    degrees = saved.shape[1]
    return pl.pallas_call(
        middle_kernel,
        grid=(orders // GROUP,),
        in_specs=[
            pl.BlockSpec((GROUP * GROUP, GROUP * GROUP), lambda i: (0, 0)),
            pl.BlockSpec((2, lats, GROUP, width), lambda i: (0, 0, i, 0)),
            pl.BlockSpec((2, degrees, GROUP, width), lambda i: (0, 0, i, 0)),
            pl.BlockSpec((2, degrees, width), lambda i: (0, 0, 0)),
            pl.BlockSpec((GROUP, lats, degrees), lambda i: (i, 0, 0)),
        ],
        out_specs=[
            pl.BlockSpec((2, degrees, width), lambda i: (0, 0, 0)),
            pl.BlockSpec((2, lats, GROUP, width), lambda i: (0, 0, i, 0)),
        ],
        out_shape=[
            jax.ShapeDtypeStruct((2, degrees, width), jnp.float32),
            jax.ShapeDtypeStruct(order_major.shape, jnp.bfloat16),
        ],
        scratch_shapes=[
            pltpu.VMEM((GROUP, lats, 2 * width), jnp.bfloat16),
            pltpu.VMEM((GROUP, degrees, 2 * width), jnp.bfloat16),
            pltpu.VMEM((GROUP, lats, 2 * width), jnp.bfloat16),
        ],
        compiler_params=pltpu.CompilerParams(vmem_limit_bytes=48 << 20),
        cost_estimate=pl.CostEstimate(
            flops=8 * lats * orders * degrees * width,
            bytes_accessed=saved.size * 2 + order_major.size * 4,
            transcendentals=0,
        ),
    )(swap_matrix(), order_major, saved, weights, jnp.swapaxes(maps, 1, 2))


def middle_plain(order_major, saved, weights, maps):
    degree_grad = jnp.einsum(
        "mlt,rtmc->rlmc", maps, order_major, preferred_element_type=jnp.float32
    )
    saved = saved.astype(jnp.float32)
    filter_terms = jnp.stack(
        [
            jnp.sum(degree_grad[0] * saved[0] + degree_grad[1] * saved[1], axis=1),
            jnp.sum(degree_grad[1] * saved[0] - degree_grad[0] * saved[1], axis=1),
        ]
    )
    real, imag = weights[0][:, None, :], weights[1][:, None, :]
    coef_grad = jnp.stack(
        [
            real * degree_grad[0] + imag * degree_grad[1],
            real * degree_grad[1] - imag * degree_grad[0],
        ]
    ).astype(jnp.bfloat16)
    band_grad = jnp.einsum(
        "mlt,rlmc->rtmc", maps, coef_grad, preferred_element_type=jnp.float32
    ).astype(jnp.bfloat16)
    return filter_terms, band_grad


def shards(
    block_hidden, incoming_grad, saved_coeffs, filter_weights, up_weight, down_weight, latitude_maps
):
    band_rows = block_hidden.shape[1]
    slab_width = block_hidden.shape[2]
    embed = block_hidden.shape[3]
    token_rows = block_hidden[0].reshape(band_rows * slab_width, embed)
    grad_rows = incoming_grad[0].reshape(band_rows * slab_width, embed)
    up_matrix = up_weight[0]
    down_matrix = down_weight[0]
    pre_active = jnp.dot(token_rows, up_matrix, preferred_element_type=jnp.float32)
    activation, slopes = gelu_pair(pre_active)
    activated = activation.astype(jnp.bfloat16)
    carried = lax.dot_general(
        grad_rows, down_matrix, (((1,), (1,)), ((), ())), preferred_element_type=jnp.float32
    )
    grad_pre = (carried * slopes).astype(jnp.bfloat16)
    down_terms = lax.dot_general(
        activated, grad_rows, (((0,), (0,)), ((), ())), preferred_element_type=jnp.float32
    )
    up_terms = lax.dot_general(
        token_rows, grad_pre, (((0,), (0,)), ((), ())), preferred_element_type=jnp.float32
    )
    back_rows = lax.dot_general(
        grad_pre, up_matrix, (((1,), (1,)), ((), ())), preferred_element_type=jnp.float32
    )
    grad_hidden = (grad_rows.astype(jnp.float32) + back_rows).astype(jnp.bfloat16)
    grad_grid = grad_hidden.reshape(band_rows, slab_width, embed)
    group_count = lax.axis_size(("lat", "lon"))
    lat_count = lax.axis_size("lat")
    lon_index = lax.axis_index("lon")
    half = embed // 2
    period = slab_width * 2
    synthesis, analysis = transform_tables(0, slab_width * 2, period, MODES)
    other = jnp.where(lon_index == 0, grad_grid[..., half:], grad_grid[..., :half])
    own = jnp.where(lon_index == 0, grad_grid[..., :half], grad_grid[..., half:])
    theirs = shifted(other, "lon", 1)
    own_start = lon_index * slab_width
    their_start = (1 - lon_index) * slab_width
    own_table = lax.dynamic_slice_in_dim(synthesis, own_start, slab_width, 1)
    their_table = lax.dynamic_slice_in_dim(synthesis, their_start, slab_width, 1)
    spectrum = jnp.einsum(
        "tkc,rkm->rtmc",
        jnp.concatenate([own, theirs], axis=1),
        jnp.concatenate([own_table, their_table], axis=1),
        preferred_element_type=jnp.float32,
    ).astype(jnp.bfloat16)
    order_major = lax.all_to_all(spectrum, "lat", split_axis=2, concat_axis=1, tiled=True)
    mixer_terms = jnp.stack([up_terms, down_terms]).astype(jnp.bfloat16)
    mixer_terms = mixer_terms.reshape(2, group_count, -1, up_terms.shape[1])
    mixer_parts = lax.all_to_all(mixer_terms, ("lat", "lon"), split_axis=1, concat_axis=1, tiled=True)
    up_grad, down_grad = jnp.sum(mixer_parts.astype(jnp.float32), axis=1)
    fits = order_major.shape[2] % GROUP == 0 and order_major.shape[1] <= 64
    filter_terms, band_grad = (middle if fits else middle_plain)(
        order_major, saved_coeffs[0], filter_weights[0], latitude_maps
    )
    band_major = lax.all_to_all(band_grad, "lat", split_axis=1, concat_axis=2, tiled=True)
    filter_terms = filter_terms.reshape(2, lat_count, -1, half).astype(jnp.bfloat16)
    filter_parts = lax.all_to_all(filter_terms, "lat", split_axis=1, concat_axis=1, tiled=True)
    filter_grad = jnp.sum(filter_parts.astype(jnp.float32), axis=1)

    def back(start):
        table = lax.dynamic_slice_in_dim(analysis, start, slab_width, 1)
        return jnp.einsum(
            "rtmc,rkm->tkc", band_major, table, preferred_element_type=jnp.float32
        ).astype(jnp.bfloat16)

    their_back = shifted(back(their_start), "lon", 1)
    own_back = back(own_start)
    grid_back = jnp.concatenate(
        [
            jnp.where(lon_index == 0, own_back, their_back),
            jnp.where(lon_index == 0, their_back, own_back),
        ],
        axis=2,
    )
    passed = (grad_grid.astype(jnp.float32) + grid_back.astype(jnp.float32)).astype(jnp.bfloat16)
    handed_grad = shifted(passed[None], "section", 1)
    return (handed_grad, filter_grad[None], up_grad[None], down_grad[None])


def solution(mesh):
    in_specs = (
        P("section", "lat", "lon", None),
        P("section", "lat", "lon", None),
        P("section", None, None, "lat", "lon"),
        P("section", None, None, "lon"),
        P("section", None, None),
        P("section", None, None),
        P("lat", None, None),
    )
    out_specs = (
        P("section", "lat", "lon", None),
        P("section", None, "lat", "lon"),
        P("section", ("lat", "lon"), None),
        P("section", ("lat", "lon"), None),
    )
    return jax.shard_map(shards, mesh=mesh, in_specs=in_specs, out_specs=out_specs, check_vma=False)
```

```python
import math

import jax
import jax.numpy as jnp
import numpy as np
from jax import lax
from jax.experimental import pallas as pl
from jax.experimental.pallas import tpu as pltpu
from jax.sharding import PartitionSpec as P

MODES = 384


def shifted(block, axis, distance):
    devices = range(lax.axis_size(axis))
    route = [((i - distance) % len(devices), i) for i in devices]
    return lax.ppermute(block, axis, route)


def transform_tables(period, orders_kept):
    positions = np.arange(period, dtype=np.int32)
    orders = np.arange(orders_kept, dtype=np.int32)
    phases = positions[:, None] * orders[None, :] % period
    angles = phases.astype(np.float32) * np.float32(2.0 * math.pi / period)
    factor = np.float32(1.0 / math.sqrt(period))
    cosine = np.cos(angles) * factor
    sine_part = np.sin(angles) * factor
    doubled = np.where(orders == 0, 1.0, 2.0).astype(np.float32)[None, :]
    synthesis = np.stack([cosine * doubled, -sine_part * doubled]).astype(jnp.bfloat16)
    analysis = np.stack([cosine, -sine_part]).astype(jnp.bfloat16)
    return (synthesis, analysis)


def gelu_pair(pre_active):
    normal_cdf = 0.5 * (1.0 + lax.erf(pre_active * (1.0 / math.sqrt(2.0))))
    density = jnp.exp(-0.5 * pre_active * pre_active) * (1.0 / math.sqrt(2.0 * math.pi))
    return (pre_active * normal_cdf, normal_cdf + pre_active * density)

GROUP = 16


def swap_matrix():
    row = lax.broadcasted_iota(jnp.int32, (GROUP * GROUP, GROUP * GROUP), 0)
    column = lax.broadcasted_iota(jnp.int32, (GROUP * GROUP, GROUP * GROUP), 1)
    partner = row % GROUP * GROUP + row // GROUP
    return jnp.where(partner == column, 1.0, 0.0).astype(jnp.bfloat16)


def swapped(matrix, block):
    flat = block.reshape(GROUP * GROUP, block.shape[2])
    turned = jnp.dot(matrix, flat, preferred_element_type=jnp.float32)
    return turned.astype(jnp.bfloat16).reshape(block.shape)


def middle_kernel(
    swap_ref, x_ref, s_ref, w_ref, map_ref, filter_ref, out_ref, x_major, s_major, out_major
):
    owners, _, lats, _, width = x_ref.shape
    bands_count = owners * lats
    degrees = s_ref.shape[1]
    step = pl.program_id(0)
    matrix = swap_ref[...]

    @pl.when(step == 0)
    def _():
        out_major[...] = jnp.zeros_like(out_major)
        for part in range(2):
            lanes = slice(part * width, (part + 1) * width)
            x_all = x_ref[:, part].reshape(bands_count, GROUP, width)
            for piece in range(bands_count // GROUP):
                rows = slice(piece * GROUP, (piece + 1) * GROUP)
                x_major[:, rows, lanes] = swapped(matrix, x_all[rows])

    for part in range(2):
        lanes = slice(part * width, (part + 1) * width)
        for piece in range(degrees // GROUP):
            rows = slice(piece * GROUP, (piece + 1) * GROUP)
            s_major[:, rows, lanes] = swapped(matrix, s_ref[part, rows])

    filter_ref[...] = jnp.zeros_like(filter_ref)

    @pl.loop(0, GROUP)
    def _(order):
        maps = map_ref[order]
        degree = lax.dot_general(
            maps, x_major[order], (((0,), (0,)), ((), ())), preferred_element_type=jnp.float32
        )
        real, imag = degree[:, :width], degree[:, width:]
        saved_real = s_major[order, :, :width].astype(jnp.float32)
        saved_imag = s_major[order, :, width:].astype(jnp.float32)
        filter_ref[0] += real * saved_real + imag * saved_imag
        filter_ref[1] += imag * saved_real - real * saved_imag
        weight_real, weight_imag = w_ref[0], w_ref[1]
        coef_real = (weight_real * real + weight_imag * imag).astype(jnp.bfloat16)
        coef_imag = (weight_real * imag - weight_imag * real).astype(jnp.bfloat16)
        out_major[order, :, :width] += jnp.dot(
            maps, coef_real, preferred_element_type=jnp.float32
        )
        out_major[order, :, width:] += jnp.dot(
            maps, coef_imag, preferred_element_type=jnp.float32
        )

    @pl.when(step == pl.num_programs(0) - 1)
    def _():
        for part in range(2):
            lanes = slice(part * width, (part + 1) * width)
            pieces = []
            for piece in range(bands_count // GROUP):
                rows = slice(piece * GROUP, (piece + 1) * GROUP)
                block = out_major[:, rows, lanes].astype(jnp.bfloat16)
                pieces.append(swapped(matrix, block))
            whole = jnp.concatenate(pieces, axis=0)
            out_ref[:, part] = whole.reshape(owners, lats, GROUP, width)


BLOCK = 384


def middle(group, bands, saved, weights, maps):
    owners, _, lats, _, width = bands.shape
    degrees = saved.shape[1]
    steps = degrees // BLOCK
    return pl.pallas_call(
        middle_kernel,
        grid=(steps,),
        in_specs=[
            pl.BlockSpec((GROUP * GROUP, GROUP * GROUP), lambda i: (0, 0)),
            pl.BlockSpec(bands.shape, lambda i: (0, 0, 0, 0, 0)),
            pl.BlockSpec((2, BLOCK, GROUP, width), lambda i: (0, i, group, 0)),
            pl.BlockSpec((2, BLOCK, width), lambda i: (0, i, 0)),
            pl.BlockSpec((GROUP, owners * lats, BLOCK), lambda i: (group, 0, i)),
        ],
        out_specs=[
            pl.BlockSpec((2, BLOCK, width), lambda i: (0, i, 0)),
            pl.BlockSpec(bands.shape, lambda i: (0, 0, 0, 0, 0)),
        ],
        out_shape=[
            jax.ShapeDtypeStruct((2, degrees, width), jnp.float32),
            jax.ShapeDtypeStruct(bands.shape, jnp.bfloat16),
        ],
        scratch_shapes=[
            pltpu.VMEM((GROUP, owners * lats, 2 * width), jnp.bfloat16),
            pltpu.VMEM((GROUP, BLOCK, 2 * width), jnp.bfloat16),
            pltpu.VMEM((GROUP, owners * lats, 2 * width), jnp.float32),
        ],
        compiler_params=pltpu.CompilerParams(vmem_limit_bytes=40 << 20),
        cost_estimate=pl.CostEstimate(
            flops=20_000_000_000, bytes_accessed=saved.size * 2 // 3, transcendentals=0
        ),
    )(swap_matrix(), bands, saved, weights, jnp.swapaxes(maps, 1, 2))


def middle_plain(group, bands, saved, weights, maps):
    owners, _, lats, orders, width = bands.shape
    order_major = jnp.swapaxes(bands, 0, 1).reshape(2, owners * lats, orders, width)
    degree_grad = jnp.einsum(
        "mlt,rtmc->rlmc", maps, order_major, preferred_element_type=jnp.float32
    )
    saved = saved.astype(jnp.float32)
    filter_terms = jnp.stack(
        [
            jnp.sum(degree_grad[0] * saved[0] + degree_grad[1] * saved[1], axis=1),
            jnp.sum(degree_grad[1] * saved[0] - degree_grad[0] * saved[1], axis=1),
        ]
    )
    real, imag = weights[0][:, None, :], weights[1][:, None, :]
    coef_grad = jnp.stack(
        [
            real * degree_grad[0] + imag * degree_grad[1],
            real * degree_grad[1] - imag * degree_grad[0],
        ]
    ).astype(jnp.bfloat16)
    band_grad = jnp.einsum(
        "mlt,rlmc->rtmc", maps, coef_grad, preferred_element_type=jnp.float32
    ).astype(jnp.bfloat16)
    band_grad = jnp.swapaxes(band_grad.reshape(2, owners, lats, orders, width), 0, 1)
    return filter_terms, band_grad


def mixer_kernel(
    hidden_ref, grad_ref, up_ref, down_ref, rows_ref, low_ref, high_ref, terms_ref, up_sum, down_sum
):
    step = pl.program_id(0)
    hidden, grad = hidden_ref[0], grad_ref[0]
    pre_active = jnp.dot(hidden, up_ref[...], preferred_element_type=jnp.float32)
    activation, slopes = gelu_pair(pre_active)
    carried = lax.dot_general(
        grad, down_ref[...], (((1,), (1,)), ((), ())), preferred_element_type=jnp.float32
    )
    grad_pre = (carried * slopes).astype(jnp.bfloat16)
    back_rows = lax.dot_general(
        grad_pre, up_ref[...], (((1,), (1,)), ((), ())), preferred_element_type=jnp.float32
    )
    grad_hidden = (grad.astype(jnp.float32) + back_rows).astype(jnp.bfloat16)
    rows_ref[0] = grad_hidden
    half = grad_hidden.shape[1] // 2
    low_ref[0] = grad_hidden[:, :half]
    high_ref[0] = grad_hidden[:, half:]

    @pl.when(step == 0)
    def _():
        up_sum[...] = jnp.zeros_like(up_sum)
        down_sum[...] = jnp.zeros_like(down_sum)

    across = (((0,), (0,)), ((), ()))
    up_sum[...] += lax.dot_general(hidden, grad_pre, across, preferred_element_type=jnp.float32)
    down_sum[...] += lax.dot_general(
        activation.astype(jnp.bfloat16), grad, across, preferred_element_type=jnp.float32
    )

    @pl.when(step == pl.num_programs(0) - 1)
    def _():
        terms_ref[0] = up_sum[...].astype(jnp.bfloat16)
        terms_ref[1] = down_sum[...].astype(jnp.bfloat16)


def mixer(hidden, grad, up_matrix, down_matrix):
    lats, longitudes, embed = hidden.shape
    units = up_matrix.shape[1]
    rows = pl.BlockSpec((1, longitudes, embed), lambda i: (i, 0, 0))
    halves = pl.BlockSpec((1, longitudes, embed // 2), lambda i: (i, 0, 0))
    return pl.pallas_call(
        mixer_kernel,
        grid=(lats,),
        in_specs=[
            rows,
            rows,
            pl.BlockSpec(up_matrix.shape, lambda i: (0, 0)),
            pl.BlockSpec(down_matrix.shape, lambda i: (0, 0)),
        ],
        out_specs=[rows, halves, halves, pl.BlockSpec((2, embed, units), lambda i: (0, 0, 0))],
        out_shape=[
            jax.ShapeDtypeStruct(hidden.shape, jnp.bfloat16),
            jax.ShapeDtypeStruct((lats, longitudes, embed // 2), jnp.bfloat16),
            jax.ShapeDtypeStruct((lats, longitudes, embed // 2), jnp.bfloat16),
            jax.ShapeDtypeStruct((2, embed, units), jnp.bfloat16),
        ],
        scratch_shapes=[
            pltpu.VMEM((embed, units), jnp.float32),
            pltpu.VMEM((units, embed), jnp.float32),
        ],
        compiler_params=pltpu.CompilerParams(vmem_limit_bytes=40 << 20),
    )(hidden, grad, up_matrix, down_matrix)


def back_kernel(table_ref, *refs):
    *bands, near_ref, far_ref = refs
    owners, _, _, orders, width = bands[0].shape
    stacked = jnp.concatenate(
        [ref[:, :, 0].reshape(owners * 2 * orders, width) for ref in bands], axis=0
    )
    length = near_ref.shape[1]
    far_ref[0] = jnp.dot(
        table_ref[length:], stacked, preferred_element_type=jnp.float32
    ).astype(jnp.bfloat16)
    near_ref[0] = jnp.dot(
        table_ref[:length], stacked, preferred_element_type=jnp.float32
    ).astype(jnp.bfloat16)


def back(table, bands):
    owners, _, lats, orders, width = bands[0].shape
    period = table.shape[0]
    out = pl.BlockSpec((1, period // 2, width), lambda i: (i, 0, 0))
    shape = jax.ShapeDtypeStruct((lats, period // 2, width), jnp.bfloat16)
    block = pl.BlockSpec((owners, 2, 1, orders, width), lambda i: (0, 0, i, 0, 0))
    return pl.pallas_call(
        back_kernel,
        grid=(lats,),
        in_specs=[pl.BlockSpec(table.shape, lambda i: (0, 0))] + [block] * len(bands),
        out_specs=[out, out],
        out_shape=[shape, shape],
        compiler_params=pltpu.CompilerParams(vmem_limit_bytes=40 << 20),
    )(table, *bands)


def back_plain(table, bands):
    stacked = jnp.concatenate(
        [jnp.transpose(x, (2, 0, 1, 3, 4)).reshape(x.shape[2], -1, x.shape[4]) for x in bands],
        axis=1,
    )
    whole = jnp.einsum("kq,tqc->tkc", table, stacked, preferred_element_type=jnp.float32)
    whole = whole.astype(jnp.bfloat16)
    length = table.shape[0] // 2
    return whole[:, :length], whole[:, length:]


def shards(
    block_hidden, incoming_grad, saved_coeffs, filter_weights, up_weight, down_weight, latitude_maps
):
    band_rows = block_hidden.shape[1]
    slab_width = block_hidden.shape[2]
    embed = block_hidden.shape[3]
    grad_grid, low, high, mixer_terms = mixer(
        block_hidden[0], incoming_grad[0], up_weight[0], down_weight[0]
    )
    group_count = lax.axis_size(("lat", "lon"))
    lat_count = lax.axis_size("lat")
    lon_index = lax.axis_index("lon")
    half = embed // 2
    period = slab_width * 2
    local_orders = latitude_maps.shape[0]
    fits = local_orders % GROUP == 0 and band_rows * lat_count <= 64
    width = GROUP if fits else local_orders
    groups = local_orders // width
    synthesis, analysis = transform_tables(period, MODES)

    def rolled(table):
        table = jnp.asarray(np.concatenate([table, table[:slab_width]], axis=0))
        return lax.dynamic_slice_in_dim(table, lon_index * slab_width, period, 0)

    def by_group(table):
        return table.reshape(2, period, lat_count, groups, width).transpose(1, 3, 2, 0, 4)

    other = jnp.where(lon_index == 0, high, low)
    own = jnp.where(lon_index == 0, low, high)
    theirs = shifted(other, "lon", 1)
    handed_rows = shifted(grad_grid, "section", 1)
    all_rows = jnp.concatenate([own, theirs], axis=1)
    synthesis = rolled(by_group(synthesis))
    analysis = rolled(by_group(analysis).reshape(period, -1))
    bands, filter_terms = [], 0.0
    for group in range(groups):
        spectrum = jnp.einsum(
            "tkc,kdrj->drtjc", all_rows, synthesis[:, group], preferred_element_type=jnp.float32
        ).astype(jnp.bfloat16)
        bands.append(lax.all_to_all(spectrum, "lat", split_axis=0, concat_axis=0, tiled=True))
    returned = []
    flipped = []
    for group in range(groups):
        if group == 1:
            bands[1], last_bands = lax.optimization_barrier((bands[1], back_bands))
            back_bands = last_bands
        if group >= 1:
            flipped.append(shifted(back_bands, "section", 1))
        if group == 2:
            bands[2], flipped[0], handed_rows = lax.optimization_barrier(
                (bands[2], flipped[0], handed_rows)
            )
        if group >= 2:
            returned.append(
                lax.all_to_all(flipped[group - 2], "lat", split_axis=0, concat_axis=0, tiled=True)
            )
        terms, back_bands = (middle if fits else middle_plain)(
            group, bands[group], saved_coeffs[0], filter_weights[0], latitude_maps
        )
        filter_terms = filter_terms + terms
    if returned:
        back_bands, returned[-1] = lax.optimization_barrier((back_bands, returned[-1]))
    flipped.append(shifted(back_bands, "section", 1))
    for block in flipped[len(returned) :]:
        returned.append(lax.all_to_all(block, "lat", split_axis=0, concat_axis=0, tiled=True))
    filter_terms = filter_terms.reshape(2, lat_count, -1, half).astype(jnp.bfloat16)
    mixer_terms, filter_terms, returned[-1] = lax.optimization_barrier(
        (mixer_terms, filter_terms, returned[-1])
    )
    filter_parts = lax.all_to_all(filter_terms, "lat", split_axis=1, concat_axis=1, tiled=True)
    filter_grad = jnp.sum(filter_parts.astype(jnp.float32), axis=1)
    mixer_terms = mixer_terms.reshape(2, group_count, -1, mixer_terms.shape[2])
    mixer_parts = lax.all_to_all(mixer_terms, ("lat", "lon"), split_axis=1, concat_axis=1, tiled=True)
    up_grad, down_grad = jnp.sum(mixer_parts.astype(jnp.float32), axis=1)
    own_back, for_other = (back if fits else back_plain)(analysis, returned)
    their_back = shifted(for_other, "lon", 1)
    grid_back = jnp.concatenate(
        [
            jnp.where(lon_index == 0, own_back, their_back),
            jnp.where(lon_index == 0, their_back, own_back),
        ],
        axis=2,
    )
    passed = handed_rows.astype(jnp.float32) + grid_back.astype(jnp.float32)
    handed_grad = passed.astype(jnp.bfloat16)[None]
    return (handed_grad, filter_grad[None], up_grad[None], down_grad[None])


def solution(mesh):
    in_specs = (
        P("section", "lat", "lon", None),
        P("section", "lat", "lon", None),
        P("section", None, None, "lat", "lon"),
        P("section", None, None, "lon"),
        P("section", None, None),
        P("section", None, None),
        P("lat", None, None),
    )
    out_specs = (
        P("section", "lat", "lon", None),
        P("section", None, "lat", "lon"),
        P("section", ("lat", "lon"), None),
        P("section", ("lat", "lon"), None),
    )
    return jax.shard_map(shards, mesh=mesh, in_specs=in_specs, out_specs=out_specs, check_vma=False)
```

```python
import math

import jax
import jax.numpy as jnp
import numpy as np
from jax import lax
from jax.experimental import pallas as pl
from jax.experimental.pallas import tpu as pltpu
from jax.sharding import PartitionSpec as P

MODES = 384


def shifted(block, axis, distance):
    devices = range(lax.axis_size(axis))
    route = [((i - distance) % len(devices), i) for i in devices]
    return lax.ppermute(block, axis, route)


def transform_tables(period, orders_kept):
    positions = np.arange(period, dtype=np.int32)
    orders = np.arange(orders_kept, dtype=np.int32)
    phases = positions[:, None] * orders[None, :] % period
    angles = phases.astype(np.float32) * np.float32(2.0 * math.pi / period)
    factor = np.float32(1.0 / math.sqrt(period))
    cosine = np.cos(angles) * factor
    sine_part = np.sin(angles) * factor
    doubled = np.where(orders == 0, 1.0, 2.0).astype(np.float32)[None, :]
    synthesis = np.stack([cosine * doubled, -sine_part * doubled]).astype(jnp.bfloat16)
    analysis = np.stack([cosine, -sine_part]).astype(jnp.bfloat16)
    return (synthesis, analysis)


def gelu_pair(pre_active):
    normal_cdf = 0.5 * (1.0 + lax.erf(pre_active * (1.0 / math.sqrt(2.0))))
    density = jnp.exp(-0.5 * pre_active * pre_active) * (1.0 / math.sqrt(2.0 * math.pi))
    return (pre_active * normal_cdf, normal_cdf + pre_active * density)

GROUP = 16


def swap_matrix():
    row = lax.broadcasted_iota(jnp.int32, (GROUP * GROUP, GROUP * GROUP), 0)
    column = lax.broadcasted_iota(jnp.int32, (GROUP * GROUP, GROUP * GROUP), 1)
    partner = row % GROUP * GROUP + row // GROUP
    return jnp.where(partner == column, 1.0, 0.0).astype(jnp.bfloat16)


def swapped(matrix, block):
    flat = block.reshape(GROUP * GROUP, block.shape[2])
    turned = jnp.dot(matrix, flat, preferred_element_type=jnp.float32)
    return turned.astype(jnp.bfloat16).reshape(block.shape)


def middle_kernel(
    swap_ref, x_ref, s_ref, w_ref, map_ref, filter_ref, out_ref, x_major, s_major, out_major
):
    owners, _, lats, _, width = x_ref.shape
    bands_count = owners * lats
    degrees = s_ref.shape[1]
    step = pl.program_id(0)
    matrix = swap_ref[...]

    @pl.when(step == 0)
    def _():
        out_major[...] = jnp.zeros_like(out_major)
        for part in range(2):
            lanes = slice(part * width, (part + 1) * width)
            x_all = x_ref[:, part].reshape(bands_count, GROUP, width)
            for piece in range(bands_count // GROUP):
                rows = slice(piece * GROUP, (piece + 1) * GROUP)
                x_major[:, rows, lanes] = swapped(matrix, x_all[rows])

    for part in range(2):
        lanes = slice(part * width, (part + 1) * width)
        for piece in range(degrees // GROUP):
            rows = slice(piece * GROUP, (piece + 1) * GROUP)
            s_major[:, rows, lanes] = swapped(matrix, s_ref[part, rows])

    filter_ref[...] = jnp.zeros_like(filter_ref)

    @pl.loop(0, GROUP)
    def _(order):
        maps = map_ref[order]
        degree = lax.dot_general(
            maps, x_major[order], (((0,), (0,)), ((), ())), preferred_element_type=jnp.float32
        )
        real, imag = degree[:, :width], degree[:, width:]
        saved_real = s_major[order, :, :width].astype(jnp.float32)
        saved_imag = s_major[order, :, width:].astype(jnp.float32)
        filter_ref[0] += real * saved_real + imag * saved_imag
        filter_ref[1] += imag * saved_real - real * saved_imag
        weight_real, weight_imag = w_ref[0], w_ref[1]
        coef_real = (weight_real * real + weight_imag * imag).astype(jnp.bfloat16)
        coef_imag = (weight_real * imag - weight_imag * real).astype(jnp.bfloat16)
        out_major[order, :, :width] += jnp.dot(
            maps, coef_real, preferred_element_type=jnp.float32
        )
        out_major[order, :, width:] += jnp.dot(
            maps, coef_imag, preferred_element_type=jnp.float32
        )

    @pl.when(step == pl.num_programs(0) - 1)
    def _():
        for part in range(2):
            lanes = slice(part * width, (part + 1) * width)
            pieces = []
            for piece in range(bands_count // GROUP):
                rows = slice(piece * GROUP, (piece + 1) * GROUP)
                block = out_major[:, rows, lanes].astype(jnp.bfloat16)
                pieces.append(swapped(matrix, block))
            whole = jnp.concatenate(pieces, axis=0)
            out_ref[:, part] = whole.reshape(owners, lats, GROUP, width)


BLOCK = 384


def middle(group, bands, saved, weights, maps):
    owners, _, lats, _, width = bands.shape
    degrees = saved.shape[1]
    steps = degrees // BLOCK
    return pl.pallas_call(
        middle_kernel,
        grid=(steps,),
        in_specs=[
            pl.BlockSpec((GROUP * GROUP, GROUP * GROUP), lambda i: (0, 0)),
            pl.BlockSpec(bands.shape, lambda i: (0, 0, 0, 0, 0)),
            pl.BlockSpec((2, BLOCK, GROUP, width), lambda i: (0, i, group, 0)),
            pl.BlockSpec((2, BLOCK, width), lambda i: (0, i, 0)),
            pl.BlockSpec((GROUP, owners * lats, BLOCK), lambda i: (group, 0, i)),
        ],
        out_specs=[
            pl.BlockSpec((2, BLOCK, width), lambda i: (0, i, 0)),
            pl.BlockSpec(bands.shape, lambda i: (0, 0, 0, 0, 0)),
        ],
        out_shape=[
            jax.ShapeDtypeStruct((2, degrees, width), jnp.float32),
            jax.ShapeDtypeStruct(bands.shape, jnp.bfloat16),
        ],
        scratch_shapes=[
            pltpu.VMEM((GROUP, owners * lats, 2 * width), jnp.bfloat16),
            pltpu.VMEM((GROUP, BLOCK, 2 * width), jnp.bfloat16),
            pltpu.VMEM((GROUP, owners * lats, 2 * width), jnp.float32),
        ],
        compiler_params=pltpu.CompilerParams(vmem_limit_bytes=40 << 20),
        cost_estimate=pl.CostEstimate(
            flops=20_000_000_000, bytes_accessed=saved.size * 2 // 3, transcendentals=0
        ),
    )(swap_matrix(), bands, saved, weights, jnp.swapaxes(maps, 1, 2))


def middle_plain(group, bands, saved, weights, maps):
    owners, _, lats, orders, width = bands.shape
    order_major = jnp.swapaxes(bands, 0, 1).reshape(2, owners * lats, orders, width)
    degree_grad = jnp.einsum(
        "mlt,rtmc->rlmc", maps, order_major, preferred_element_type=jnp.float32
    )
    saved = saved.astype(jnp.float32)
    filter_terms = jnp.stack(
        [
            jnp.sum(degree_grad[0] * saved[0] + degree_grad[1] * saved[1], axis=1),
            jnp.sum(degree_grad[1] * saved[0] - degree_grad[0] * saved[1], axis=1),
        ]
    )
    real, imag = weights[0][:, None, :], weights[1][:, None, :]
    coef_grad = jnp.stack(
        [
            real * degree_grad[0] + imag * degree_grad[1],
            real * degree_grad[1] - imag * degree_grad[0],
        ]
    ).astype(jnp.bfloat16)
    band_grad = jnp.einsum(
        "mlt,rlmc->rtmc", maps, coef_grad, preferred_element_type=jnp.float32
    ).astype(jnp.bfloat16)
    band_grad = jnp.swapaxes(band_grad.reshape(2, owners, lats, orders, width), 0, 1)
    return filter_terms, band_grad


def mixer_kernel(
    hidden_ref, grad_ref, up_ref, down_ref, rows_ref, low_ref, high_ref, terms_ref, up_sum, down_sum
):
    step = pl.program_id(0)
    hidden, grad = hidden_ref[0], grad_ref[0]
    pre_active = jnp.dot(hidden, up_ref[...], preferred_element_type=jnp.float32)
    activation, slopes = gelu_pair(pre_active)
    carried = lax.dot_general(
        grad, down_ref[...], (((1,), (1,)), ((), ())), preferred_element_type=jnp.float32
    )
    grad_pre = (carried * slopes).astype(jnp.bfloat16)
    back_rows = lax.dot_general(
        grad_pre, up_ref[...], (((1,), (1,)), ((), ())), preferred_element_type=jnp.float32
    )
    grad_hidden = (grad.astype(jnp.float32) + back_rows).astype(jnp.bfloat16)
    rows_ref[0] = grad_hidden
    half = grad_hidden.shape[1] // 2
    low_ref[0] = grad_hidden[:, :half]
    high_ref[0] = grad_hidden[:, half:]

    @pl.when(step == 0)
    def _():
        up_sum[...] = jnp.zeros_like(up_sum)
        down_sum[...] = jnp.zeros_like(down_sum)

    across = (((0,), (0,)), ((), ()))
    up_sum[...] += lax.dot_general(hidden, grad_pre, across, preferred_element_type=jnp.float32)
    down_sum[...] += lax.dot_general(
        activation.astype(jnp.bfloat16), grad, across, preferred_element_type=jnp.float32
    )

    @pl.when(step == pl.num_programs(0) - 1)
    def _():
        terms_ref[0] = up_sum[...].astype(jnp.bfloat16)
        terms_ref[1] = down_sum[...].astype(jnp.bfloat16)


def mixer(hidden, grad, up_matrix, down_matrix):
    lats, longitudes, embed = hidden.shape
    units = up_matrix.shape[1]
    rows = pl.BlockSpec((1, longitudes, embed), lambda i: (i, 0, 0))
    halves = pl.BlockSpec((1, longitudes, embed // 2), lambda i: (i, 0, 0))
    return pl.pallas_call(
        mixer_kernel,
        grid=(lats,),
        in_specs=[
            rows,
            rows,
            pl.BlockSpec(up_matrix.shape, lambda i: (0, 0)),
            pl.BlockSpec(down_matrix.shape, lambda i: (0, 0)),
        ],
        out_specs=[rows, halves, halves, pl.BlockSpec((2, embed, units), lambda i: (0, 0, 0))],
        out_shape=[
            jax.ShapeDtypeStruct(hidden.shape, jnp.bfloat16),
            jax.ShapeDtypeStruct((lats, longitudes, embed // 2), jnp.bfloat16),
            jax.ShapeDtypeStruct((lats, longitudes, embed // 2), jnp.bfloat16),
            jax.ShapeDtypeStruct((2, embed, units), jnp.bfloat16),
        ],
        scratch_shapes=[
            pltpu.VMEM((embed, units), jnp.float32),
            pltpu.VMEM((units, embed), jnp.float32),
        ],
        compiler_params=pltpu.CompilerParams(vmem_limit_bytes=40 << 20),
    )(hidden, grad, up_matrix, down_matrix)


def back_kernel(table_ref, *refs):
    *bands, near_ref, far_ref = refs
    owners, _, _, orders, width = bands[0].shape
    stacked = jnp.concatenate(
        [ref[:, :, 0].reshape(owners * 2 * orders, width) for ref in bands], axis=0
    )
    length = near_ref.shape[1]
    far_ref[0] = jnp.dot(
        table_ref[length:], stacked, preferred_element_type=jnp.float32
    ).astype(jnp.bfloat16)
    near_ref[0] = jnp.dot(
        table_ref[:length], stacked, preferred_element_type=jnp.float32
    ).astype(jnp.bfloat16)


def back(table, bands):
    owners, _, lats, orders, width = bands[0].shape
    period = table.shape[0]
    out = pl.BlockSpec((1, period // 2, width), lambda i: (i, 0, 0))
    shape = jax.ShapeDtypeStruct((lats, period // 2, width), jnp.bfloat16)
    block = pl.BlockSpec((owners, 2, 1, orders, width), lambda i: (0, 0, i, 0, 0))
    return pl.pallas_call(
        back_kernel,
        grid=(lats,),
        in_specs=[pl.BlockSpec(table.shape, lambda i: (0, 0))] + [block] * len(bands),
        out_specs=[out, out],
        out_shape=[shape, shape],
        compiler_params=pltpu.CompilerParams(vmem_limit_bytes=40 << 20),
    )(table, *bands)


def back_plain(table, bands):
    stacked = jnp.concatenate(
        [jnp.transpose(x, (2, 0, 1, 3, 4)).reshape(x.shape[2], -1, x.shape[4]) for x in bands],
        axis=1,
    )
    whole = jnp.einsum("kq,tqc->tkc", table, stacked, preferred_element_type=jnp.float32)
    whole = whole.astype(jnp.bfloat16)
    length = table.shape[0] // 2
    return whole[:, :length], whole[:, length:]


def shards(
    block_hidden, incoming_grad, saved_coeffs, filter_weights, up_weight, down_weight, latitude_maps
):
    band_rows = block_hidden.shape[1]
    slab_width = block_hidden.shape[2]
    embed = block_hidden.shape[3]
    grad_grid, low, high, mixer_terms = mixer(
        block_hidden[0], incoming_grad[0], up_weight[0], down_weight[0]
    )
    lat_count = lax.axis_size("lat")
    lon_index = lax.axis_index("lon")
    half = embed // 2
    period = slab_width * 2
    local_orders = latitude_maps.shape[0]
    fits = local_orders % GROUP == 0 and band_rows * lat_count <= 64
    width = GROUP if fits else local_orders
    groups = local_orders // width
    synthesis, analysis = transform_tables(period, MODES)

    def rolled(table):
        table = jnp.asarray(np.concatenate([table, table[:slab_width]], axis=0))
        return lax.dynamic_slice_in_dim(table, lon_index * slab_width, period, 0)

    def by_group(table):
        return table.reshape(2, period, lat_count, groups, width).transpose(1, 3, 2, 0, 4)

    other = jnp.where(lon_index == 0, high, low)
    own = jnp.where(lon_index == 0, low, high)
    theirs = shifted(other, "lon", 1)
    handed_rows = shifted(grad_grid, "section", 1)
    all_rows = jnp.concatenate([own, theirs], axis=1)
    synthesis = rolled(by_group(synthesis))
    analysis = rolled(by_group(analysis).reshape(period, -1))
    unit_half = mixer_terms.shape[2] // 2
    mixer_terms = mixer_terms.reshape(2, lat_count, 2, -1, 2 * unit_half)
    mixer_other = jnp.where(lon_index == 0, mixer_terms[:, :, 1], mixer_terms[:, :, 0])
    mixer_own = jnp.where(lon_index == 0, mixer_terms[:, :, 0], mixer_terms[:, :, 1])
    mixer_theirs = shifted(mixer_other, "lon", 1)

    def spread(block):
        return lax.all_to_all(block, "lat", split_axis=0, concat_axis=0, tiled=True)

    def run(group, block):
        return (middle if fits else middle_plain)(
            group, block, saved_coeffs[0], filter_weights[0], latitude_maps
        )

    def ordered(*values):
        return lax.optimization_barrier(values)

    spectra = []
    for group in range(groups):
        spectra.append(
            jnp.einsum(
                "tkc,kdrj->drtjc", all_rows, synthesis[:, group], preferred_element_type=jnp.float32
            ).astype(jnp.bfloat16)
        )
    arriving = [spread(block) for block in spectra[:2]]
    filter_terms, flipped, returned = 0.0, [], []
    for group in range(groups):
        if group == 1:
            arriving[1], handed_rows = ordered(arriving[1], handed_rows)
        terms, out = run(group, arriving[group])
        filter_terms = filter_terms + terms
        if group + 2 < groups:
            block, out = ordered(spectra[group + 2], out)
            arriving.append(spread(block))
        if group + 1 < groups:
            arriving[group + 1], out = ordered(arriving[group + 1], out)
        if group >= 1:
            flipped[-1], out = ordered(flipped[-1], out)
            if returned:
                flipped[-1], returned[-1] = ordered(flipped[-1], returned[-1])
            returned.append(spread(flipped[-1]))
        flipped.append(shifted(out, "section", 1))
    if returned:
        flipped[-1], returned[-1] = ordered(flipped[-1], returned[-1])
    returned.append(spread(flipped[-1]))
    mixer_sum = (mixer_own.astype(jnp.float32) + mixer_theirs.astype(jnp.float32)).astype(
        jnp.bfloat16
    )
    mixer_sum = jnp.swapaxes(mixer_sum, 0, 1).reshape(lat_count, -1, 2 * unit_half)
    share = mixer_sum.shape[1]
    filter_terms = filter_terms.reshape(2, lat_count, -1, half).astype(jnp.bfloat16)
    filter_terms = jnp.swapaxes(filter_terms, 0, 1).reshape(lat_count, -1, half)
    totals = jnp.concatenate(
        [mixer_sum[..., :unit_half], mixer_sum[..., unit_half:], filter_terms], axis=1
    )
    totals, returned[-1] = ordered(totals, returned[-1])
    totals = jnp.sum(spread(totals).astype(jnp.float32), axis=0)
    mixer_total = jnp.concatenate([totals[:share], totals[share : 2 * share]], axis=1)
    up_grad, down_grad = mixer_total[: share // 2], mixer_total[share // 2 :]
    filter_grad = totals[2 * share :].reshape(2, -1, half)
    own_back, for_other = (back if fits else back_plain)(analysis, returned)
    their_back = shifted(for_other, "lon", 1)
    grid_back = jnp.concatenate(
        [
            jnp.where(lon_index == 0, own_back, their_back),
            jnp.where(lon_index == 0, their_back, own_back),
        ],
        axis=2,
    )
    passed = handed_rows.astype(jnp.float32) + grid_back.astype(jnp.float32)
    handed_grad = passed.astype(jnp.bfloat16)[None]
    return (handed_grad, filter_grad[None], up_grad[None], down_grad[None])


def solution(mesh):
    in_specs = (
        P("section", "lat", "lon", None),
        P("section", "lat", "lon", None),
        P("section", None, None, "lat", "lon"),
        P("section", None, None, "lon"),
        P("section", None, None),
        P("section", None, None),
        P("lat", None, None),
    )
    out_specs = (
        P("section", "lat", "lon", None),
        P("section", None, "lat", "lon"),
        P("section", ("lat", "lon"), None),
        P("section", ("lat", "lon"), None),
    )
    return jax.shard_map(shards, mesh=mesh, in_specs=in_specs, out_specs=out_specs, check_vma=False)
```

```python
import math

import jax
import jax.numpy as jnp
import numpy as np
from jax import lax
from jax.experimental import pallas as pl
from jax.experimental.pallas import tpu as pltpu
from jax.sharding import PartitionSpec as P

MODES = 384


def shifted(block, axis, distance):
    devices = range(lax.axis_size(axis))
    route = [((i - distance) % len(devices), i) for i in devices]
    return lax.ppermute(block, axis, route)


def transform_tables(period, orders_kept):
    positions = np.arange(period, dtype=np.int32)
    orders = np.arange(orders_kept, dtype=np.int32)
    phases = positions[:, None] * orders[None, :] % period
    angles = phases.astype(np.float32) * np.float32(2.0 * math.pi / period)
    factor = np.float32(1.0 / math.sqrt(period))
    cosine = np.cos(angles) * factor
    sine_part = np.sin(angles) * factor
    doubled = np.where(orders == 0, 1.0, 2.0).astype(np.float32)[None, :]
    synthesis = np.stack([cosine * doubled, -sine_part * doubled]).astype(jnp.bfloat16)
    analysis = np.stack([cosine, -sine_part]).astype(jnp.bfloat16)
    return (synthesis, analysis)


def gelu_pair(pre_active):
    normal_cdf = 0.5 * (1.0 + lax.erf(pre_active * (1.0 / math.sqrt(2.0))))
    density = jnp.exp(-0.5 * pre_active * pre_active) * (1.0 / math.sqrt(2.0 * math.pi))
    return (pre_active * normal_cdf, normal_cdf + pre_active * density)

GROUP = 16


def swap_matrix():
    row = lax.broadcasted_iota(jnp.int32, (GROUP * GROUP, GROUP * GROUP), 0)
    column = lax.broadcasted_iota(jnp.int32, (GROUP * GROUP, GROUP * GROUP), 1)
    partner = row % GROUP * GROUP + row // GROUP
    return jnp.where(partner == column, 1.0, 0.0).astype(jnp.bfloat16)


def swapped(matrix, block):
    flat = block.reshape(GROUP * GROUP, block.shape[2])
    turned = jnp.dot(matrix, flat, preferred_element_type=jnp.float32)
    return turned.astype(jnp.bfloat16).reshape(block.shape)


def middle_kernel(
    swap_ref, x_ref, s_ref, w_ref, map_ref, filter_ref, out_ref, x_major, s_major, out_major
):
    owners, _, lats, _, width = x_ref.shape
    bands_count = owners * lats
    degrees = s_ref.shape[1]
    step = pl.program_id(0)
    matrix = swap_ref[...]

    @pl.when(step == 0)
    def _():
        out_major[...] = jnp.zeros_like(out_major)
        for part in range(2):
            lanes = slice(part * width, (part + 1) * width)
            x_all = x_ref[:, part].reshape(bands_count, GROUP, width)
            for piece in range(bands_count // GROUP):
                rows = slice(piece * GROUP, (piece + 1) * GROUP)
                x_major[:, rows, lanes] = swapped(matrix, x_all[rows])

    for part in range(2):
        lanes = slice(part * width, (part + 1) * width)
        for piece in range(degrees // GROUP):
            rows = slice(piece * GROUP, (piece + 1) * GROUP)
            s_major[:, rows, lanes] = swapped(matrix, s_ref[part, rows])

    filter_ref[...] = jnp.zeros_like(filter_ref)

    @pl.loop(0, GROUP)
    def _(order):
        maps = map_ref[order]
        degree = lax.dot_general(
            maps, x_major[order], (((0,), (0,)), ((), ())), preferred_element_type=jnp.float32
        )
        real, imag = degree[:, :width], degree[:, width:]
        saved_real = s_major[order, :, :width].astype(jnp.float32)
        saved_imag = s_major[order, :, width:].astype(jnp.float32)
        filter_ref[0] += real * saved_real + imag * saved_imag
        filter_ref[1] += imag * saved_real - real * saved_imag
        weight_real, weight_imag = w_ref[0], w_ref[1]
        coef_real = (weight_real * real + weight_imag * imag).astype(jnp.bfloat16)
        coef_imag = (weight_real * imag - weight_imag * real).astype(jnp.bfloat16)
        out_major[order, :, :width] += jnp.dot(
            maps, coef_real, preferred_element_type=jnp.float32
        )
        out_major[order, :, width:] += jnp.dot(
            maps, coef_imag, preferred_element_type=jnp.float32
        )

    @pl.when(step == pl.num_programs(0) - 1)
    def _():
        for part in range(2):
            lanes = slice(part * width, (part + 1) * width)
            pieces = []
            for piece in range(bands_count // GROUP):
                rows = slice(piece * GROUP, (piece + 1) * GROUP)
                block = out_major[:, rows, lanes].astype(jnp.bfloat16)
                pieces.append(swapped(matrix, block))
            whole = jnp.concatenate(pieces, axis=0)
            out_ref[:, part] = whole.reshape(owners, lats, GROUP, width)


BLOCK = 384


def middle(group, bands, saved, weights, maps):
    owners, _, lats, _, width = bands.shape
    degrees = saved.shape[1]
    steps = degrees // BLOCK
    return pl.pallas_call(
        middle_kernel,
        grid=(steps,),
        in_specs=[
            pl.BlockSpec((GROUP * GROUP, GROUP * GROUP), lambda i: (0, 0)),
            pl.BlockSpec(bands.shape, lambda i: (0, 0, 0, 0, 0)),
            pl.BlockSpec((2, BLOCK, GROUP, width), lambda i: (0, i, group, 0)),
            pl.BlockSpec((2, BLOCK, width), lambda i: (0, i, 0)),
            pl.BlockSpec((GROUP, owners * lats, BLOCK), lambda i: (group, 0, i)),
        ],
        out_specs=[
            pl.BlockSpec((2, BLOCK, width), lambda i: (0, i, 0)),
            pl.BlockSpec(bands.shape, lambda i: (0, 0, 0, 0, 0)),
        ],
        out_shape=[
            jax.ShapeDtypeStruct((2, degrees, width), jnp.float32),
            jax.ShapeDtypeStruct(bands.shape, jnp.bfloat16),
        ],
        scratch_shapes=[
            pltpu.VMEM((GROUP, owners * lats, 2 * width), jnp.bfloat16),
            pltpu.VMEM((GROUP, BLOCK, 2 * width), jnp.bfloat16),
            pltpu.VMEM((GROUP, owners * lats, 2 * width), jnp.float32),
        ],
        compiler_params=pltpu.CompilerParams(vmem_limit_bytes=40 << 20),
        cost_estimate=pl.CostEstimate(
            flops=20_000_000_000, bytes_accessed=saved.size * 2 // 3, transcendentals=0
        ),
    )(swap_matrix(), bands, saved, weights, jnp.swapaxes(maps, 1, 2))


def middle_plain(group, bands, saved, weights, maps):
    owners, _, lats, orders, width = bands.shape
    order_major = jnp.swapaxes(bands, 0, 1).reshape(2, owners * lats, orders, width)
    degree_grad = jnp.einsum(
        "mlt,rtmc->rlmc", maps, order_major, preferred_element_type=jnp.float32
    )
    saved = saved.astype(jnp.float32)
    filter_terms = jnp.stack(
        [
            jnp.sum(degree_grad[0] * saved[0] + degree_grad[1] * saved[1], axis=1),
            jnp.sum(degree_grad[1] * saved[0] - degree_grad[0] * saved[1], axis=1),
        ]
    )
    real, imag = weights[0][:, None, :], weights[1][:, None, :]
    coef_grad = jnp.stack(
        [
            real * degree_grad[0] + imag * degree_grad[1],
            real * degree_grad[1] - imag * degree_grad[0],
        ]
    ).astype(jnp.bfloat16)
    band_grad = jnp.einsum(
        "mlt,rlmc->rtmc", maps, coef_grad, preferred_element_type=jnp.float32
    ).astype(jnp.bfloat16)
    band_grad = jnp.swapaxes(band_grad.reshape(2, owners, lats, orders, width), 0, 1)
    return filter_terms, band_grad


def mixer_kernel(
    hidden_ref, grad_ref, up_ref, down_ref, rows_ref, low_ref, high_ref, terms_ref, up_sum, down_sum
):
    step = pl.program_id(0)
    hidden, grad = hidden_ref[0], grad_ref[0]
    pre_active = jnp.dot(hidden, up_ref[...], preferred_element_type=jnp.float32)
    activation, slopes = gelu_pair(pre_active)
    carried = lax.dot_general(
        grad, down_ref[...], (((1,), (1,)), ((), ())), preferred_element_type=jnp.float32
    )
    grad_pre = (carried * slopes).astype(jnp.bfloat16)
    back_rows = lax.dot_general(
        grad_pre, up_ref[...], (((1,), (1,)), ((), ())), preferred_element_type=jnp.float32
    )
    grad_hidden = (grad.astype(jnp.float32) + back_rows).astype(jnp.bfloat16)
    rows_ref[0] = grad_hidden
    half = grad_hidden.shape[1] // 2
    low_ref[0] = grad_hidden[:, :half]
    high_ref[0] = grad_hidden[:, half:]

    @pl.when(step == 0)
    def _():
        up_sum[...] = jnp.zeros_like(up_sum)
        down_sum[...] = jnp.zeros_like(down_sum)

    across = (((0,), (0,)), ((), ()))
    up_sum[...] += lax.dot_general(hidden, grad_pre, across, preferred_element_type=jnp.float32)
    down_sum[...] += lax.dot_general(
        activation.astype(jnp.bfloat16), grad, across, preferred_element_type=jnp.float32
    )

    @pl.when(step == pl.num_programs(0) - 1)
    def _():
        terms_ref[0] = up_sum[...].astype(jnp.bfloat16)
        terms_ref[1] = down_sum[...].astype(jnp.bfloat16)


def mixer(hidden, grad, up_matrix, down_matrix):
    lats, longitudes, embed = hidden.shape
    units = up_matrix.shape[1]
    rows = pl.BlockSpec((1, longitudes, embed), lambda i: (i, 0, 0))
    halves = pl.BlockSpec((1, longitudes, embed // 2), lambda i: (i, 0, 0))
    return pl.pallas_call(
        mixer_kernel,
        grid=(lats,),
        in_specs=[
            rows,
            rows,
            pl.BlockSpec(up_matrix.shape, lambda i: (0, 0)),
            pl.BlockSpec(down_matrix.shape, lambda i: (0, 0)),
        ],
        out_specs=[rows, halves, halves, pl.BlockSpec((2, embed, units), lambda i: (0, 0, 0))],
        out_shape=[
            jax.ShapeDtypeStruct(hidden.shape, jnp.bfloat16),
            jax.ShapeDtypeStruct((lats, longitudes, embed // 2), jnp.bfloat16),
            jax.ShapeDtypeStruct((lats, longitudes, embed // 2), jnp.bfloat16),
            jax.ShapeDtypeStruct((2, embed, units), jnp.bfloat16),
        ],
        scratch_shapes=[
            pltpu.VMEM((embed, units), jnp.float32),
            pltpu.VMEM((units, embed), jnp.float32),
        ],
        compiler_params=pltpu.CompilerParams(vmem_limit_bytes=40 << 20),
    )(hidden, grad, up_matrix, down_matrix)


def back_kernel(table_ref, *refs):
    *bands, near_ref, far_ref = refs
    owners, _, _, orders, width = bands[0].shape
    stacked = jnp.concatenate(
        [ref[:, :, 0].reshape(owners * 2 * orders, width) for ref in bands], axis=0
    )
    length = near_ref.shape[1]
    far_ref[0] = jnp.dot(
        table_ref[length:], stacked, preferred_element_type=jnp.float32
    ).astype(jnp.bfloat16)
    near_ref[0] = jnp.dot(
        table_ref[:length], stacked, preferred_element_type=jnp.float32
    ).astype(jnp.bfloat16)


def back(table, bands):
    owners, _, lats, orders, width = bands[0].shape
    period = table.shape[0]
    out = pl.BlockSpec((1, period // 2, width), lambda i: (i, 0, 0))
    shape = jax.ShapeDtypeStruct((lats, period // 2, width), jnp.bfloat16)
    block = pl.BlockSpec((owners, 2, 1, orders, width), lambda i: (0, 0, i, 0, 0))
    return pl.pallas_call(
        back_kernel,
        grid=(lats,),
        in_specs=[pl.BlockSpec(table.shape, lambda i: (0, 0))] + [block] * len(bands),
        out_specs=[out, out],
        out_shape=[shape, shape],
        compiler_params=pltpu.CompilerParams(vmem_limit_bytes=40 << 20),
    )(table, *bands)


def back_plain(table, bands):
    stacked = jnp.concatenate(
        [jnp.transpose(x, (2, 0, 1, 3, 4)).reshape(x.shape[2], -1, x.shape[4]) for x in bands],
        axis=1,
    )
    whole = jnp.einsum("kq,tqc->tkc", table, stacked, preferred_element_type=jnp.float32)
    whole = whole.astype(jnp.bfloat16)
    length = table.shape[0] // 2
    return whole[:, :length], whole[:, length:]


def shards(
    block_hidden, incoming_grad, saved_coeffs, filter_weights, up_weight, down_weight, latitude_maps
):
    band_rows = block_hidden.shape[1]
    slab_width = block_hidden.shape[2]
    embed = block_hidden.shape[3]
    grad_grid, low, high, mixer_terms = mixer(
        block_hidden[0], incoming_grad[0], up_weight[0], down_weight[0]
    )
    lat_count = lax.axis_size("lat")
    lon_index = lax.axis_index("lon")
    half = embed // 2
    period = slab_width * 2
    local_orders = latitude_maps.shape[0]
    fits = local_orders % GROUP == 0 and band_rows * lat_count <= 64
    width = GROUP if fits else local_orders
    groups = local_orders // width
    synthesis, analysis = transform_tables(period, MODES)

    def rolled(table):
        table = jnp.asarray(np.concatenate([table, table[:slab_width]], axis=0))
        return lax.dynamic_slice_in_dim(table, lon_index * slab_width, period, 0)

    def by_group(table):
        return table.reshape(2, period, lat_count, groups, width).transpose(1, 3, 2, 0, 4)

    other = jnp.where(lon_index == 0, high, low)
    own = jnp.where(lon_index == 0, low, high)
    theirs = shifted(other, "lon", 1)
    handed_rows = shifted(grad_grid, "section", 1)
    all_rows = jnp.concatenate([own, theirs], axis=1)
    synthesis = rolled(by_group(synthesis))
    analysis = rolled(by_group(analysis).reshape(period, -1))
    unit_half = mixer_terms.shape[2] // 2
    mixer_terms = mixer_terms.reshape(2, lat_count, 2, -1, 2 * unit_half)
    mixer_other = jnp.where(lon_index == 0, mixer_terms[:, :, 1], mixer_terms[:, :, 0])
    mixer_own = jnp.where(lon_index == 0, mixer_terms[:, :, 0], mixer_terms[:, :, 1])
    mixer_theirs = shifted(mixer_other, "lon", 1)

    def spread(block):
        return lax.all_to_all(block, "lat", split_axis=0, concat_axis=0, tiled=True)

    def run(group, block):
        return (middle if fits else middle_plain)(
            group, block, saved_coeffs[0], filter_weights[0], latitude_maps
        )

    def ordered(*values):
        return lax.optimization_barrier(values)

    mixer_sum = (mixer_own.astype(jnp.float32) + mixer_theirs.astype(jnp.float32)).astype(
        jnp.bfloat16
    )
    mixer_sum = jnp.swapaxes(mixer_sum, 0, 1).reshape(lat_count, -1, 2 * unit_half)
    share = mixer_sum.shape[1]
    mixer_sum = jnp.concatenate([mixer_sum[..., :unit_half], mixer_sum[..., unit_half:]], axis=1)
    spectra = []
    for group in range(groups):
        spectra.append(
            jnp.einsum(
                "tkc,kdrj->drtjc", all_rows, synthesis[:, group], preferred_element_type=jnp.float32
            ).astype(jnp.bfloat16)
        )
    arriving = [spread(block) for block in spectra[:2]]
    filter_terms, flipped, returned = 0.0, [], []
    for group in range(groups):
        if group == 1:
            arriving[1], handed_rows = ordered(arriving[1], handed_rows)
        terms, out = run(group, arriving[group])
        filter_terms = filter_terms + terms
        if group == 0:
            mixer_sum, arriving[-1], out = ordered(mixer_sum, arriving[-1], out)
            mixer_parts = spread(mixer_sum)
        if group + 2 < groups:
            block, out = ordered(spectra[group + 2], out)
            if group == 0:
                block, mixer_parts = ordered(block, mixer_parts)
            arriving.append(spread(block))
        if group + 1 < groups:
            arriving[group + 1], out = ordered(arriving[group + 1], out)
        if group >= 1:
            flipped[-1], out = ordered(flipped[-1], out)
            if returned:
                flipped[-1], returned[-1] = ordered(flipped[-1], returned[-1])
            returned.append(spread(flipped[-1]))
        flipped.append(shifted(out, "section", 1))
    if returned:
        flipped[-1], returned[-1] = ordered(flipped[-1], returned[-1])
    returned.append(spread(flipped[-1]))
    filter_terms = filter_terms.reshape(2, lat_count, -1, half).astype(jnp.bfloat16)
    filter_terms = jnp.swapaxes(filter_terms, 0, 1).reshape(lat_count, -1, half)
    filter_terms, returned[-1] = ordered(filter_terms, returned[-1])
    filter_grad = jnp.sum(spread(filter_terms).astype(jnp.float32), axis=0).reshape(2, -1, half)
    totals = jnp.sum(mixer_parts.astype(jnp.float32), axis=0)
    mixer_total = jnp.concatenate([totals[:share], totals[share:]], axis=1)
    up_grad, down_grad = mixer_total[: share // 2], mixer_total[share // 2 :]
    own_back, for_other = (back if fits else back_plain)(analysis, returned)
    their_back = shifted(for_other, "lon", 1)
    grid_back = jnp.concatenate(
        [
            jnp.where(lon_index == 0, own_back, their_back),
            jnp.where(lon_index == 0, their_back, own_back),
        ],
        axis=2,
    )
    passed = handed_rows.astype(jnp.float32) + grid_back.astype(jnp.float32)
    handed_grad = passed.astype(jnp.bfloat16)[None]
    return (handed_grad, filter_grad[None], up_grad[None], down_grad[None])


def solution(mesh):
    in_specs = (
        P("section", "lat", "lon", None),
        P("section", "lat", "lon", None),
        P("section", None, None, "lat", "lon"),
        P("section", None, None, "lon"),
        P("section", None, None),
        P("section", None, None),
        P("lat", None, None),
    )
    out_specs = (
        P("section", "lat", "lon", None),
        P("section", None, "lat", "lon"),
        P("section", ("lat", "lon"), None),
        P("section", ("lat", "lon"), None),
    )
    return jax.shard_map(shards, mesh=mesh, in_specs=in_specs, out_specs=out_specs, check_vma=False)
```
